256 devices in a mesh: expert: 64 (over y, z, core), blk: 4 (over x).
Axes of the slice: x: 4, y: 4, z: 8, core: 2. Of those that a mesh axis runs over, the one named last changes fastest.
Arguments:
- activations: bfloat16 [131072, 2048], P(('expert', 'blk')), may hold values from -6 to 6
- destination: int32 [16384, 1], P(('expert', 'blk')), may hold values from 0 to 63; in each aligned block of 64 rows (0 to 63, 64 to 127, ...) at most 2 rows name the same one
Outputs:
- hessian: float32 [64, 2048, 2048], P('expert', 'blk')
The draws below stay inside these ranges and needn't reach their ends.
Inputs may be any that keep to these rules, and one draw needn't show every extreme that they name: `destination`: among the 64 blocks of one device (aligned runs of 64 entries), no expert is named more than 2 times, a bound that the blocks of some device reach; every expert is named somewhere.
All inputs are finite; a program needn't handle non-finite values.
Results may differ from the reference program's by a relative error of at most 0.0003.
Values may be sent and summed in bfloat16 or wider, within the bound.
No kernel may reach another device: no remote copies, remote signals or barrier semaphores. Data moves between devices by JAX's collectives and lax.ppermute only.
A program may use at most 128 MiB of HBM per device.

```python
import math
import jax
import jax.numpy as jnp
import numpy as np
from jax import lax

FFE = 2048
BLK = 8
NB = 64
EXPERTS = 64
CAP = 2
NBLOCKS = 16384
N_EXPERT = 64
N_BLK = 4


def block_scale(rng, shape, pieces, least, largest):
    gain, own = 1.0, jax.random.fold_in(rng, 6)
    for dim, parts in pieces:
        draws = jnp.exp(jax.random.uniform(jax.random.fold_in(own, dim), (parts,), jnp.float32, least / len(pieces), largest / len(pieces)))
        gain = gain * jnp.repeat(draws, shape[dim] // parts).reshape([-1 if axis == dim else 1 for axis in range(len(shape))])
    return gain


def deal_out(stream_key, own, number, rows, amount, top, reach, lean):
    sequence = jax.random.permutation(stream_key, amount)
    packed, ordinary = load_shares(amount, rows * top, reach, lean, True), load_shares(amount, rows * top, reach, lean, False)
    places = jnp.arange(amount)

    def named(sizes, turn):
        used = int((sizes > 0).sum())
        fixed = max(1, used // 4)
        passed = fixed + (places - fixed + turn * (used - fixed)) % max(1, amount - fixed)
        return jnp.zeros((amount,), jnp.int32).at[sequence[jnp.where(places < fixed, places, passed)]].set(jnp.asarray(sizes, jnp.int32))

    sizes = jnp.where(number % 4 == 0, named(packed, number // 4), named(ordinary, number - number // 4 - 1))
    mixed = jax.random.permutation(jax.random.fold_in(own, 3), amount)
    giver, taker = mixed[0:amount // 2 * 2:2], mixed[1:amount // 2 * 2:2]
    slack = jnp.minimum(sizes[giver] - 1, reach - sizes[taker]) // 2
    slack = jnp.where((giver == sequence[0]) | (taker == sequence[0]) | (sizes[taker] == 0), 0, jnp.maximum(slack, 0))
    passed = jax.random.randint(jax.random.fold_in(own, 4), (amount // 2,), 0, 1 << 20) % (slack + 1)
    sizes = sizes.at[giver].add(-passed).at[taker].add(passed)
    labels = jnp.searchsorted(jnp.cumsum(sizes), jnp.arange(rows * top), side="right").astype(jnp.int32)
    listing = labels.reshape(top, rows).T
    listing = listing[jax.random.permutation(jax.random.fold_in(own, 1), rows)]
    turn = jax.random.randint(jax.random.fold_in(own, 2), (rows, 1), 0, top)
    return jnp.take_along_axis(listing, (jnp.arange(top)[None, :] + turn) % top, axis=1)


def load_shares(amount, total, most, slope, full):
    weights = [(1 << 20) // math.isqrt(grade ** slope) + 1 for grade in range(1, amount + 1)]
    largest = most if full else min(most, max(-(-total // amount), total * weights[0] // sum(weights)))
    least = 1 if total - largest >= amount - 1 else 0
    counts, spare = [largest] + [least] * (amount - 1), total - largest - least * (amount - 1)
    while spare > 0:
        candidates = [i for i in range(1, amount) if counts[i] < largest] or [i for i in range(1, amount) if counts[i] < most]
        pool, budget = sum([weights[i] for i in candidates]), spare
        for i in candidates:
            extra = min(most - counts[i], max(1, budget * weights[i] // pool), spare)
            counts[i] = counts[i] + extra
            spare = spare - extra
    return np.array(counts)


def noise(rng, extent, spread, most, split=(), kind=jnp.bfloat16):
    values = spread * jax.random.normal(rng, extent, jnp.float32)
    if split:
        values = values * block_scale(rng, extent, split, -0.22, 0.18)
    return jnp.clip(values, -most, most).astype(kind)


def setup_inputs(seed: int = 0) -> dict:
    key_list = jax.random.split(jax.random.key(seed), 3)
    activations = noise(key_list[0], (NBLOCKS * BLK, FFE), 1.0, 6.0, ((0, 256),))
    destination_keys = jax.random.split(jax.random.fold_in(key_list[1], 1), NBLOCKS // NB)
    destination_turns = jax.random.permutation(jax.random.fold_in(key_list[1], 3), NBLOCKS // NB)
    destination = jax.vmap(lambda own, number: deal_out(jax.random.fold_in(key_list[1], 2), own, number, NB, EXPERTS, 1, CAP, 2))(destination_keys, destination_turns).reshape((NBLOCKS, 1))
    return dict(activations=activations, destination=destination)


def reference(activations, destination):
    targets = destination[:, 0].astype(jnp.int32)
    block_total = targets.shape[0]
    most_blocks = N_EXPERT * N_BLK * CAP
    expert_ids = jnp.arange(EXPERTS, dtype=jnp.int32)
    block_counts = jnp.sum((targets[None, :] == expert_ids[:, None]).astype(jnp.int32), axis=1).astype(jnp.int32)
    starts = (jnp.cumsum(block_counts) - block_counts).astype(jnp.int32)
    ordering = jnp.argsort(targets, stable=True)
    blocks = activations.reshape(block_total, BLK, FFE)[ordering]
    padded = jnp.concatenate([blocks, jnp.zeros((most_blocks, BLK, FFE), activations.dtype)], axis=0)

    def one_expert(expert_id):
        start = starts[expert_id]
        taken = block_counts[expert_id]
        segment = lax.dynamic_slice_in_dim(padded, start, most_blocks, 0)
        keep = (jnp.arange(most_blocks, dtype=jnp.int32) < taken)[:, None, None]
        rows_kept = jnp.where(keep, segment, jnp.zeros_like(segment)).reshape(most_blocks * BLK, FFE)
        gram = lax.dot_general(rows_kept, rows_kept, (((0,), (0,)), ((), ())), preferred_element_type=jnp.float32)
        return gram * (2.0 / (BLK * taken.astype(jnp.float32)))

    return lax.map(one_expert, expert_ids)
```

```python
import functools

import jax
import jax.numpy as jnp
from jax import lax
from jax.experimental import pallas as pl
from jax.experimental.pallas import tpu as pltpu
from jax.sharding import PartitionSpec as P

FIRST = 384
WIRE = jnp.float16
NOTE = 16
MARK = 64.0
TOP = 8192.0


def rows_dot(left, right):
    return lax.dot_general(
        left, right, (((0,), (0,)), ((), ())), preferred_element_type=jnp.float32
    )


def write_note(out_ref, place, rows, facts_ref):
    shape = (NOTE, out_ref.shape[-1])
    row = lax.broadcasted_iota(jnp.int32, shape, 0)
    note = jnp.where(row == 0, facts_ref[1], jnp.where(row == 1, facts_ref[2], facts_ref[3]))
    out_ref[place + (pl.ds(rows, NOTE),)] = note


def first_kernel(owners_ref, facts_ref, x0_ref, out_ref):
    first = x0_ref.shape[1] // 4
    half = first // 2
    scale = facts_ref[0]
    for i in range(out_ref.shape[0]):
        column = pl.multiple_of(owners_ref[i] * first, 128)
        left = x0_ref[:, pl.ds(column, first)]
        for j in range(x0_ref.shape[1] // 512):
            block = rows_dot(left, x0_ref[:, 512 * j : 512 * (j + 1)]) * scale
            out_ref[i, 0, :half, 512 * j : 512 * (j + 1)] = block[:half]
            out_ref[i, 1, :half, 512 * j : 512 * (j + 1)] = block[half:]
        write_note(out_ref, (i, 0), half, facts_ref)
        write_note(out_ref, (i, 1), half, facts_ref)


def second_kernel(owners_ref, facts_ref, x0_ref, x1_ref, out_ref):
    first = x0_ref.shape[1] // 4
    last = x1_ref.shape[1] // 4
    scale = facts_ref[0]
    for i in range(out_ref.shape[0]):
        left0 = x0_ref[:, pl.ds(pl.multiple_of(owners_ref[i] * first, 128), first)]
        left1 = x1_ref[:, pl.ds(pl.multiple_of(owners_ref[i] * last, 128), last)]
        out_ref[i, 0, :first] = rows_dot(left0, x1_ref[...]) * scale
        corner = rows_dot(left1, x1_ref[...]) * scale
        out_ref[i, 0, first : first + last // 2] = corner[: last // 2]
        out_ref[i, 1, : last // 2] = corner[last // 2 :]
        for j in range(x0_ref.shape[1] // 512):
            row = last // 2 + last * j
            block = rows_dot(left1, x0_ref[:, 512 * j : 512 * (j + 1)]) * scale
            out_ref[i, 1, row : row + last] = block
        write_note(out_ref, (i, 0), first + last // 2, facts_ref)
        write_note(out_ref, (i, 1), first + last // 2, facts_ref)


def partial_grams(kernel, rows, wide, owners, facts, *arrays):
    count = owners.shape[0]
    shape = (count, 2, rows + NOTE, wide)
    smem = pl.BlockSpec(memory_space=pltpu.SMEM)
    vmem = pl.BlockSpec(memory_space=pltpu.VMEM)
    flops = 4 * count * rows * wide * arrays[0].shape[0]
    return pl.pallas_call(
        kernel,
        out_shape=jax.ShapeDtypeStruct(shape, jnp.float32),
        in_specs=[smem, smem] + [vmem] * len(arrays),
        out_specs=vmem,
        compiler_params=pltpu.CompilerParams(vmem_limit_bytes=40 * 1024 * 1024),
        cost_estimate=pl.CostEstimate(flops=flops, bytes_accessed=4 << 20, transcendentals=0),
    )(owners, facts, *arrays)


def note_of(got):
    rows = got.shape[0] - NOTE
    return tuple(got[rows + i : rows + i + 1].astype(jnp.float32) for i in range(3))


def fourth(value):
    return (value * value) * (value * value)


class Ring:
    def __init__(self, grams, facts, ranks):
        self.grams, self.ranks = grams, ranks
        self.coarse, self.fine, self.count = facts[1], facts[2], facts[3]
        self.unit = fourth(self.coarse * self.fine)

    def send(self, values, step):
        pairs = [(i, (i + step) % self.ranks) for i in range(self.ranks)]
        return lax.ppermute(values.astype(WIRE), "blk", pairs)

    def start(self):
        far = self.grams((2,))[0]
        self.far = self.send(far[0], 1), self.send(far[1], -1)
        self.near = self.grams((1, -1))
        self.direct = self.send(self.near[0, 1], 1), self.send(self.near[1, 0], -1)

    def merge(self, mine, got):
        coarse, fine, count = note_of(got)
        unit = fourth(coarse * fine)
        larger = jnp.maximum(unit, self.unit)
        row = lax.broadcasted_iota(jnp.int32, mine.shape, 0)
        rows = mine.shape[0] - NOTE
        both = mine * (self.unit / larger) + got.astype(jnp.float32) * (unit / larger)
        coarse = jnp.where(unit > self.unit, coarse, self.coarse)
        fine = jnp.where(unit > self.unit, fine, self.fine)
        note = jnp.where(row == rows, coarse, jnp.where(row == rows + 1, fine, self.count + count))
        return jnp.where(row < rows, both, note)

    def pass_on(self):
        self.merged = (
            self.send(self.merge(self.near[0, 0], self.far[0]), 1),
            self.send(self.merge(self.near[1, 1], self.far[1]), -1),
        )

    def total(self):
        own = self.grams((0,))[0]
        rows = own.shape[1] - NOTE
        halves = []
        for half, parts in (
            (0, (self.merged[0], self.direct[1])),
            (1, (self.direct[0], self.merged[1])),
        ):
            value = own[half, :rows] * self.unit
            for got in parts:
                coarse, fine, _ = note_of(got)
                value = value + got[:rows].astype(jnp.float32) * fourth(coarse * fine)
            halves.append(value * (1.0 / TOP))
        return halves, self.count + note_of(self.merged[0])[2] + note_of(self.direct[1])[2]


def on_device(activations, destination):
    targets = destination[:, 0]
    block_count = targets.shape[0]
    rows, width = activations.shape
    block_rows = rows // block_count
    groups = lax.axis_size("expert")
    ranks = lax.axis_size("blk")
    strip = width // ranks
    last = strip - FIRST
    capacity = 2
    slot_rows = groups * capacity * block_rows
    me = lax.axis_index("blk")

    positions = jnp.arange(block_count, dtype=jnp.int32)
    same_target = targets[:, None] == targets[None, :]
    earlier = positions[None, :] < positions[:, None]
    ranking = jnp.sum((same_target & earlier).astype(jnp.int32), axis=1)
    slots = targets * capacity + ranking
    row_slots = (
        slots[:, None] * block_rows + jnp.arange(block_rows, dtype=jnp.int32)[None, :]
    ).reshape(rows)
    chosen = row_slots[None, :] == jnp.arange(slot_rows, dtype=jnp.int32)[:, None]
    empty = 1.0 - jnp.sum(chosen.astype(jnp.float32), axis=1)
    selector = chosen.astype(jnp.bfloat16)

    def packed(start, stop, marked):
        cols = jnp.concatenate(
            [activations[:, d * strip + start : d * strip + stop] for d in range(ranks)], axis=1
        )
        placed = jnp.dot(selector, cols, preferred_element_type=jnp.float32)
        if marked:
            column = lax.broadcasted_iota(jnp.int32, placed.shape, 1)
            placed = placed + jnp.where(column == 0, MARK, 0.0) * empty[:, None]
        return placed.astype(jnp.bfloat16).reshape(groups, capacity * block_rows, cols.shape[1])

    def routed(x):
        got = lax.all_to_all(x, "expert", split_axis=0, concat_axis=0, tiled=True)
        return got.reshape(slot_rows, got.shape[2])

    def largest(x):
        return jnp.maximum(jnp.max(jnp.abs(x)).astype(jnp.float32), 1e-12)

    def facts_of(top, count):
        quarter = jnp.ceil(0.5 * jnp.log2(top) + 1e-3 + 0.25 * slot_rows.bit_length())
        coarse = jnp.clip(quarter, -14.0, 15.0)
        fine = jnp.clip(quarter - coarse, -14.0, 0.0)
        coarse, fine = jnp.exp2(coarse), jnp.exp2(fine)
        return jnp.stack([TOP / fourth(coarse * fine), coarse, fine, count])

    def owners(offsets):
        return jnp.stack([lax.rem(me + o + ranks, ranks) for o in offsets])

    x0 = routed(packed(0, FIRST, True))
    x0, later = lax.optimization_barrier((x0, packed(FIRST, strip, False)))
    x1 = routed(later)

    corner = x0[:, :128]
    is_mark = (corner > MARK / 2) & (lax.broadcasted_iota(jnp.int32, corner.shape, 1) == 0)
    empty_blocks = jnp.sum(is_mark.astype(jnp.float32)) / block_rows
    x0 = lax.dynamic_update_slice(x0, jnp.where(is_mark, jnp.zeros_like(corner), corner), (0, 0))

    top0 = largest(x0)
    facts0 = facts_of(top0, empty_blocks)
    ring0 = Ring(
        lambda offsets: partial_grams(
            first_kernel, FIRST // 2, ranks * FIRST, owners(offsets), facts0, x0
        ),
        facts0,
        ranks,
    )
    ring0.start()
    ring0.far, x1, top0 = lax.optimization_barrier((ring0.far, x1, top0))
    facts1 = facts_of(jnp.maximum(top0, largest(x1)), jnp.float32(0))
    ring1 = Ring(
        lambda offsets: partial_grams(
            second_kernel, FIRST + last // 2, ranks * last, owners(offsets), facts1, x0, x1
        ),
        facts1,
        ranks,
    )
    ring0.pass_on()
    ring1.start()
    ring1.pass_on()

    sums0, empty_blocks = ring0.total()
    hessian_scale = 2.0 / (float(ranks * slot_rows) - block_rows * empty_blocks)
    out = jnp.zeros((strip, width), jnp.float32)
    for half, piece in enumerate(sums0):
        for d in range(ranks):
            part = piece[:, d * FIRST : (d + 1) * FIRST] * hessian_scale[:, :FIRST]
            out = lax.dynamic_update_slice(out, part, (half * (FIRST // 2), d * strip))
    (upper, lower), _ = ring1.total()
    columns = jnp.concatenate([upper, lower[: last // 2]])
    cross = lower[last // 2 :].reshape(3, last, ranks * last)
    cross = jnp.concatenate([cross[0], cross[1], cross[2]], axis=1)
    for d in range(ranks):
        part = columns[:, d * last : (d + 1) * last] * hessian_scale[:, :last]
        out = lax.dynamic_update_slice(out, part, (0, d * strip + FIRST))
        part = cross[:, d * FIRST : (d + 1) * FIRST] * hessian_scale[:, :FIRST]
        out = lax.dynamic_update_slice(out, part, (FIRST, d * strip))
    return out[None]


def solution(mesh):
    in_specs = (P(("expert", "blk"), None), P(("expert", "blk"), None))
    out_specs = P("expert", "blk", None)
    return jax.shard_map(
        on_device, mesh=mesh, in_specs=in_specs, out_specs=out_specs, check_vma=False
    )
```

```python
import functools
import math

import jax
import jax.numpy as jnp
from jax import lax
from jax.experimental import pallas as pl
from jax.experimental.pallas import tpu as pltpu
from jax.sharding import PartitionSpec as P

FIRST = 384
WIRE = jnp.float16
NOTE = 16
MARK = 64.0
TOP = 8192.0


def rows_dot(left, right):
    return lax.dot_general(
        left, right, (((0,), (0,)), ((), ())), preferred_element_type=jnp.float32
    )


def top_of(x_ref):
    tops = [
        jnp.max(jnp.abs(x_ref[:, 512 * j : 512 * (j + 1)]), axis=0, keepdims=True)
        for j in range(x_ref.shape[1] // 512)
    ]
    top = tops[0]
    for other in tops[1:]:
        top = jnp.maximum(top, other)
    return jnp.maximum(jnp.max(top.astype(jnp.float32), axis=1, keepdims=True), 1e-12)


def write_facts(facts_ref, top, rows, count):
    quarter = jnp.ceil((0.5 / math.log(2.0)) * jnp.log(top) + 1e-3 + 0.25 * rows.bit_length())
    coarse = jnp.clip(quarter, -14.0, 15.0)
    fine = jnp.clip(quarter - coarse, -14.0, 0.0)
    row = lax.broadcasted_iota(jnp.int32, facts_ref.shape, 0)
    unit = jnp.where(row == 1, jnp.exp2(coarse), jnp.exp2(fine))
    facts_ref[...] = jnp.where(row == 0, top, jnp.where(row < 3, unit, count))


def scale_and_notes(facts_ref, *out_refs):
    coarse, fine, count = facts_ref[1:2, :1], facts_ref[2:3, :1], facts_ref[3:4, :1]
    for ref in out_refs:
        row = lax.broadcasted_iota(jnp.int32, (NOTE, ref.shape[1]), 0)
        note = jnp.where(row == 0, coarse, jnp.where(row == 1, fine, count))
        ref[ref.shape[0] - NOTE :, :] = note
    return TOP / fourth(coarse * fine)


def first_body(owners_ref, facts_ref, x0_ref, upper_ref, lower_ref):
    first = x0_ref.shape[1] // 4
    half = first // 2
    scale = scale_and_notes(facts_ref, upper_ref, lower_ref)
    for h, ref in enumerate((upper_ref, lower_ref)):
        left = x0_ref[:, pl.ds(pl.multiple_of(owners_ref[h] * first, 128), first)]
        left = left[:, h * half : (h + 1) * half]
        for j in range(x0_ref.shape[1] // 512):
            block = rows_dot(left, x0_ref[:, 512 * j : 512 * (j + 1)])
            ref[:half, 512 * j : 512 * (j + 1)] = block * scale


def second_body(owners_ref, facts_ref, x0_ref, x1_ref, upper_ref, lower_ref):
    first = x0_ref.shape[1] // 4
    last = x1_ref.shape[1] // 4
    half = last // 2
    scale = scale_and_notes(facts_ref, upper_ref, lower_ref)
    left0 = x0_ref[:, pl.ds(pl.multiple_of(owners_ref[0] * first, 128), first)]
    left1 = x1_ref[:, pl.ds(pl.multiple_of(owners_ref[0] * last, 128), last)]
    upper_ref[:first] = rows_dot(left0, x1_ref[...]) * scale
    upper_ref[first : first + half] = rows_dot(left1, x1_ref[...])[:half] * scale
    left1 = x1_ref[:, pl.ds(pl.multiple_of(owners_ref[1] * last, 128), last)]
    lower_ref[:half] = rows_dot(left1, x1_ref[...])[half:] * scale
    for j in range(x0_ref.shape[1] // 512):
        block = rows_dot(left1, x0_ref[:, 512 * j : 512 * (j + 1)])
        lower_ref[half + last * j : half + last * (j + 1)] = block * scale


def first_far(owners_ref, corner_ref, x0_ref, upper_ref, lower_ref, facts_ref):
    marks = jnp.where(corner_ref[:, :1].astype(jnp.float32) > MARK / 2, 1.0 / 8.0, 0.0)
    count = jnp.sum(marks, axis=0, keepdims=True)
    write_facts(facts_ref, top_of(x0_ref), x0_ref.shape[0], count)
    first_body(owners_ref, facts_ref, x0_ref, upper_ref, lower_ref)


def second_far(owners_ref, before_ref, x0_ref, x1_ref, upper_ref, lower_ref, facts_ref):
    top = jnp.maximum(before_ref[:1, :1], top_of(x1_ref))
    write_facts(facts_ref, top, x0_ref.shape[0], jnp.zeros_like(top))
    second_body(owners_ref, facts_ref, x0_ref, x1_ref, upper_ref, lower_ref)


def partial_grams(kernel, rows, wide, owners, *arrays, facts=False):
    smem = pl.BlockSpec(memory_space=pltpu.SMEM)
    vmem = pl.BlockSpec(memory_space=pltpu.VMEM)
    shapes = [jax.ShapeDtypeStruct((rows + NOTE, wide), jnp.float32)] * 2
    shapes += [jax.ShapeDtypeStruct((8, 128), jnp.float32)] * facts
    return pl.pallas_call(
        kernel,
        out_shape=shapes,
        in_specs=[smem] + [vmem] * len(arrays),
        out_specs=[vmem] * len(shapes),
        compiler_params=pltpu.CompilerParams(vmem_limit_bytes=40 * 1024 * 1024),
        cost_estimate=pl.CostEstimate(flops=0, bytes_accessed=0, transcendentals=0),
    )(owners, *arrays)


def pack_kernel(marked, start, slots_ref, activations_ref, out_ref, rows_ref, placed_ref, in_sem, out_sem):
    strip = activations_ref.shape[1] // 4
    wide = out_ref.shape[1] // 4
    fetches = [
        pltpu.make_async_copy(
            activations_ref.at[:, d * strip + start : d * strip + start + wide],
            rows_ref.at[d],
            in_sem.at[d],
        )
        for d in range(4)
    ]
    for fetch in fetches:
        fetch.start()
    shape = (out_ref.shape[0], slots_ref.shape[1])
    chosen = slots_ref[...] == lax.broadcasted_iota(jnp.int32, shape, 0)
    selector = jnp.where(chosen, 1.0, 0.0).astype(jnp.bfloat16)
    stores = []
    for d in range(4):
        fetches[d].wait()
        placed = jnp.dot(selector, rows_ref[d], preferred_element_type=jnp.float32)
        if marked and d == 0:
            used = jnp.sum(jnp.where(chosen, 1.0, 0.0), axis=1, keepdims=True)
            column = lax.broadcasted_iota(jnp.int32, placed.shape, 1)
            placed = placed + jnp.where(column == 0, MARK * (1.0 - used), 0.0)
        placed_ref[d] = placed.astype(jnp.bfloat16)
        store = pltpu.make_async_copy(
            placed_ref.at[d], out_ref.at[:, d * wide : (d + 1) * wide], out_sem.at[d]
        )
        store.start()
        stores.append(store)
    for store in stores:
        store.wait()


def pack(activations, slots, rows, start, wide, marked):
    hbm = pl.BlockSpec(memory_space=pltpu.HBM)
    return pl.pallas_call(
        functools.partial(pack_kernel, marked, start),
        out_shape=jax.ShapeDtypeStruct((rows, 4 * wide), jnp.bfloat16),
        in_specs=[pl.BlockSpec(memory_space=pltpu.VMEM), hbm],
        out_specs=hbm,
        scratch_shapes=[
            pltpu.VMEM((4, activations.shape[0], wide), jnp.bfloat16),
            pltpu.VMEM((4, rows, wide), jnp.bfloat16),
            pltpu.SemaphoreType.DMA((4,)),
            pltpu.SemaphoreType.DMA((4,)),
        ],
        compiler_params=pltpu.CompilerParams(vmem_limit_bytes=60 * 1024 * 1024),
    )(slots, activations)


def copies(pieces, sem):
    started = []
    for i, (source, target) in enumerate(pieces):
        copy = pltpu.make_async_copy(source, target, sem.at[i])
        copy.start()
        started.append(copy)
    for copy in started:
        copy.wait()


def place_first(upper_ref, lower_ref, out_ref, sem):
    half, first = upper_ref.shape[0], upper_ref.shape[1] // 4
    strip = out_ref.shape[1] // 4
    copies(
        [
            (
                ref.at[:, d * first : (d + 1) * first],
                out_ref.at[h * half : (h + 1) * half, d * strip : d * strip + first],
            )
            for h, ref in enumerate((upper_ref, lower_ref))
            for d in range(4)
        ],
        sem,
    )


def place_second(upper_ref, lower_ref, before_ref, out_ref, sem):
    rows, last = upper_ref.shape[0], upper_ref.shape[1] // 4
    strip = out_ref.shape[1] // 4
    first, half = strip - last, last // 2
    pieces = []
    for d in range(4):
        column = slice(d * strip + first, (d + 1) * strip)
        pieces.append((upper_ref.at[:, d * last : (d + 1) * last], out_ref.at[:rows, column]))
        pieces.append((lower_ref.at[:half, d * last : (d + 1) * last], out_ref.at[rows:, column]))
        for j in range(4 * first // 512):
            left, right = max(d * first, 512 * j), min((d + 1) * first, 512 * (j + 1))
            if left < right:
                row = half + last * j
                source = lower_ref.at[row : row + last, left - 512 * j : right - 512 * j]
                column = d * strip - d * first
                pieces.append((source, out_ref.at[first:, left + column : right + column]))
    copies(pieces, sem)


def place(kernel, shape, upper, lower, *before):
    hbm, vmem = pl.BlockSpec(memory_space=pltpu.HBM), pl.BlockSpec(memory_space=pltpu.VMEM)
    return pl.pallas_call(
        kernel,
        out_shape=jax.ShapeDtypeStruct(shape, jnp.float32),
        in_specs=[vmem, vmem] + [hbm] * len(before),
        out_specs=hbm,
        input_output_aliases={2: 0} if before else {},
        scratch_shapes=[pltpu.SemaphoreType.DMA((16,))],
        compiler_params=pltpu.CompilerParams(vmem_limit_bytes=24 * 1024 * 1024),
    )(upper, lower, *before)


def fourth(value):
    return (value * value) * (value * value)


def note_of(got):
    rows = got.shape[0] - NOTE
    return tuple(got[rows + i : rows + i + 1].astype(jnp.float32) for i in range(3))


class Ring:
    def __init__(self, far, grams, ranks):
        self.ranks = ranks
        upper, lower, facts = far()
        self.far = self.send(upper, 1), self.send(lower, -1)
        behind, ahead = grams(facts, -1, 1)
        self.direct = self.send(ahead, 1), self.send(behind, -1)
        self.facts = facts
        far, facts = lax.optimization_barrier((self.far, facts))
        ahead, behind = grams(facts, 1, -1)
        merged = self.merge(ahead, far[0]).astype(WIRE), self.merge(behind, far[1]).astype(WIRE)
        self.direct, merged = lax.optimization_barrier((self.direct, merged))
        self.merged = self.send(merged[0], 1), self.send(merged[1], -1)
        self.own = grams(facts, 0, 0)

    def send(self, values, step):
        pairs = [(i, (i + step) % self.ranks) for i in range(self.ranks)]
        return lax.ppermute(values.astype(WIRE), "blk", pairs)

    def merge(self, mine, got):
        got_coarse, got_fine, got_count = note_of(got)
        coarse, fine, count = note_of(mine)
        got_unit, unit = fourth(got_coarse * got_fine), fourth(coarse * fine)
        larger = jnp.maximum(unit, got_unit)
        row = lax.broadcasted_iota(jnp.int32, mine.shape, 0)
        rows = mine.shape[0] - NOTE
        both = mine * (unit / larger) + got.astype(jnp.float32) * (got_unit / larger)
        coarse = jnp.where(got_unit > unit, got_coarse, coarse)
        fine = jnp.where(got_unit > unit, got_fine, fine)
        note = jnp.where(row == rows, coarse, jnp.where(row == rows + 1, fine, count + got_count))
        return jnp.where(row < rows, both, note)

    def total(self):
        own = self.own
        rows = own[0].shape[0] - NOTE
        halves = []
        for mine, parts in (
            (own[0], (self.merged[0], self.direct[1])),
            (own[1], (self.direct[0], self.merged[1])),
        ):
            value = 0.0
            count = 0.0
            for got in (mine,) + parts:
                coarse, fine, more = note_of(got)
                value = value + got[:rows].astype(jnp.float32) * fourth(coarse * fine)
                count = count + more
            halves.append(value * (1.0 / TOP))
        return halves, count


def on_device(activations, destination):
    targets = destination[:, 0]
    block_count = targets.shape[0]
    rows, width = activations.shape
    block_rows = rows // block_count
    groups = lax.axis_size("expert")
    ranks = lax.axis_size("blk")
    strip = width // ranks
    last = strip - FIRST
    capacity = 2
    slot_rows = groups * capacity * block_rows
    me = lax.axis_index("blk")

    positions = jnp.arange(block_count, dtype=jnp.int32)
    same_target = targets[:, None] == targets[None, :]
    earlier = positions[None, :] < positions[:, None]
    ranking = jnp.sum((same_target & earlier).astype(jnp.int32), axis=1)
    slots = targets * capacity + ranking
    row_slots = (
        slots[:, None] * block_rows + jnp.arange(block_rows, dtype=jnp.int32)[None, :]
    ).reshape(1, rows)

    def packed(start, stop, marked):
        placed = pack(activations, row_slots, slot_rows, start, stop - start, marked)
        return placed.reshape(groups, capacity * block_rows, placed.shape[1])

    def routed(x):
        got = lax.all_to_all(x, "expert", split_axis=0, concat_axis=0, tiled=True)
        return got.reshape(slot_rows, got.shape[2])

    def owners(offsets):
        return jnp.stack([lax.rem(me + o + ranks, ranks) for o in offsets])

    x0 = routed(packed(0, FIRST, True))
    x0, later = lax.optimization_barrier((x0, packed(FIRST, strip, False)))
    x1 = routed(later)

    corner = x0[:, :128]
    is_mark = (corner > MARK / 2) & (lax.broadcasted_iota(jnp.int32, corner.shape, 1) == 0)
    x0 = lax.dynamic_update_slice(x0, jnp.where(is_mark, jnp.zeros_like(corner), corner), (0, 0))

    def owners(offsets):
        return jnp.stack([lax.rem(me + o + ranks, ranks) for o in offsets])

    x0 = routed(packed(0, FIRST, True))
    x0, later = lax.optimization_barrier((x0, packed(FIRST, strip, False)))
    x1 = routed(later)

    corner = x0[:, :128]
    is_mark = (corner > MARK / 2) & (lax.broadcasted_iota(jnp.int32, corner.shape, 1) == 0)
    empty_blocks = jnp.sum(is_mark.astype(jnp.float32)) / block_rows
    x0 = lax.dynamic_update_slice(x0, jnp.where(is_mark, jnp.zeros_like(corner), corner), (0, 0))

    half0, half1 = FIRST // 2, FIRST + last // 2
    ring0 = Ring(
        lambda: partial_grams(
            first_far, half0, ranks * FIRST, owners((2, 2)), corner, x0, facts=True
        ),
        lambda facts, *offsets: partial_grams(
            first_body, half0, ranks * FIRST, owners(offsets), facts, x0
        ),
        ranks,
    )
    ring0.merged, x1 = lax.optimization_barrier((ring0.merged, x1))
    ring1 = Ring(
        lambda: partial_grams(
            second_far, half1, ranks * last, owners((2, 2)), ring0.facts, x0, x1, facts=True
        ),
        lambda facts, *offsets: partial_grams(
            second_body, half1, ranks * last, owners(offsets), facts, x0, x1
        ),
        ranks,
    )

    ring0.merged, _ = lax.optimization_barrier((ring0.merged, ring1.facts))
    sums0, empty_blocks = ring0.total()
    hessian_scale = 2.0 / (float(ranks * slot_rows) - block_rows * empty_blocks)
    shape = (strip, width)
    out = place(place_first, shape, *[half * hessian_scale for half in sums0])
    sums1, _ = ring1.total()
    hessian_scale = hessian_scale[:, : ranks * last]
    out = place(place_second, shape, *[half * hessian_scale for half in sums1], out)
    return out[None]


def solution(mesh):
    in_specs = (P(("expert", "blk"), None), P(("expert", "blk"), None))
    out_specs = P("expert", "blk", None)
    return jax.shard_map(
        on_device, mesh=mesh, in_specs=in_specs, out_specs=out_specs, check_vma=False
    )
```

```python
import functools
import math

import jax
import jax.numpy as jnp
from jax import lax
from jax.experimental import pallas as pl
from jax.experimental.pallas import tpu as pltpu
from jax.sharding import PartitionSpec as P

FIRST = 384
WIRE = jnp.float16
NOTE = 16
MARK = 64.0
TOP = 8192.0


def rows_dot(left, right):
    return lax.dot_general(
        left, right, (((0,), (0,)), ((), ())), preferred_element_type=jnp.float32
    )


def top_of(x_ref):
    tops = [
        jnp.max(jnp.abs(x_ref[:, 512 * j : 512 * (j + 1)]), axis=0, keepdims=True)
        for j in range(x_ref.shape[1] // 512)
    ]
    top = tops[0]
    for other in tops[1:]:
        top = jnp.maximum(top, other)
    return jnp.maximum(jnp.max(top.astype(jnp.float32), axis=1, keepdims=True), 1e-12)


def write_facts(facts_ref, top, rows, count):
    quarter = jnp.ceil((0.5 / math.log(2.0)) * jnp.log(top) + 1e-3 + 0.25 * rows.bit_length())
    coarse = jnp.clip(quarter, -14.0, 15.0)
    fine = jnp.clip(quarter - coarse, -14.0, 0.0)
    row = lax.broadcasted_iota(jnp.int32, facts_ref.shape, 0)
    unit = jnp.where(row == 1, jnp.exp2(coarse), jnp.exp2(fine))
    facts_ref[...] = jnp.where(row == 0, top, jnp.where(row < 3, unit, count))


def scale_and_notes(facts_ref, *out_refs):
    coarse, fine, count = facts_ref[1:2, :1], facts_ref[2:3, :1], facts_ref[3:4, :1]
    for ref in out_refs:
        row = lax.broadcasted_iota(jnp.int32, (NOTE, ref.shape[1]), 0)
        note = jnp.where(row == 0, coarse, jnp.where(row == 1, fine, count))
        ref[ref.shape[0] - NOTE :, :] = note
    return TOP / fourth(coarse * fine)


def first_body(owners_ref, facts_ref, x0_ref, upper_ref, lower_ref):
    first = x0_ref.shape[1] // 4
    half = first // 2
    scale = scale_and_notes(facts_ref, upper_ref, lower_ref)
    for h, ref in enumerate((upper_ref, lower_ref)):
        left = x0_ref[:, pl.ds(pl.multiple_of(owners_ref[h] * first, 128), first)]
        left = left[:, h * half : (h + 1) * half]
        for j in range(x0_ref.shape[1] // 512):
            block = rows_dot(left, x0_ref[:, 512 * j : 512 * (j + 1)])
            ref[:half, 512 * j : 512 * (j + 1)] = block * scale


def second_body(owners_ref, facts_ref, x0_ref, x1_ref, upper_ref, lower_ref):
    first = x0_ref.shape[1] // 4
    last = x1_ref.shape[1] // 4
    half = last // 2
    scale = scale_and_notes(facts_ref, upper_ref, lower_ref)
    left0 = x0_ref[:, pl.ds(pl.multiple_of(owners_ref[0] * first, 128), first)]
    left1 = x1_ref[:, pl.ds(pl.multiple_of(owners_ref[0] * last, 128), last)]
    upper_ref[:first] = rows_dot(left0, x1_ref[...]) * scale
    upper_ref[first : first + half] = rows_dot(left1, x1_ref[...])[:half] * scale
    left1 = x1_ref[:, pl.ds(pl.multiple_of(owners_ref[1] * last, 128), last)]
    lower_ref[:half] = rows_dot(left1, x1_ref[...])[half:] * scale
    for j in range(x0_ref.shape[1] // 512):
        block = rows_dot(left1, x0_ref[:, 512 * j : 512 * (j + 1)])
        lower_ref[half + last * j : half + last * (j + 1)] = block * scale


def first_far(owners_ref, corner_ref, x0_ref, upper_ref, lower_ref, facts_ref):
    marks = jnp.where(corner_ref[:, :1].astype(jnp.float32) > MARK / 2, 1.0 / 8.0, 0.0)
    count = jnp.sum(marks, axis=0, keepdims=True)
    write_facts(facts_ref, top_of(x0_ref), x0_ref.shape[0], count)
    first_body(owners_ref, facts_ref, x0_ref, upper_ref, lower_ref)


def second_far(owners_ref, before_ref, x0_ref, x1_ref, upper_ref, lower_ref, facts_ref):
    top = jnp.maximum(before_ref[:1, :1], top_of(x1_ref))
    write_facts(facts_ref, top, x0_ref.shape[0], jnp.zeros_like(top))
    second_body(owners_ref, facts_ref, x0_ref, x1_ref, upper_ref, lower_ref)


def partial_grams(kernel, rows, wide, owners, *arrays, facts=False):
    smem = pl.BlockSpec(memory_space=pltpu.SMEM)
    vmem = pl.BlockSpec(memory_space=pltpu.VMEM)
    shapes = [jax.ShapeDtypeStruct((rows + NOTE, wide), jnp.float32)] * 2
    shapes += [jax.ShapeDtypeStruct((8, 128), jnp.float32)] * facts
    return pl.pallas_call(
        kernel,
        out_shape=shapes,
        in_specs=[smem] + [vmem] * len(arrays),
        out_specs=[vmem] * len(shapes),
        compiler_params=pltpu.CompilerParams(vmem_limit_bytes=40 * 1024 * 1024),
        cost_estimate=pl.CostEstimate(flops=0, bytes_accessed=0, transcendentals=0),
    )(owners, *arrays)


def pack_kernel(
    marked, start, across_ref, down_ref, activations_ref, out_ref, rows_ref, placed_ref, in_sem, out_sem
):
    strip = activations_ref.shape[1] // 4
    wide = out_ref.shape[1] // 4
    fetches = [
        pltpu.make_async_copy(
            activations_ref.at[:, d * strip + start : d * strip + start + wide],
            rows_ref.at[d],
            in_sem.at[d],
        )
        for d in range(4)
    ]
    for fetch in fetches:
        fetch.start()
    blocks, rows = across_ref.shape[1], activations_ref.shape[0]
    block_rows = rows // blocks
    earlier = lax.broadcasted_iota(jnp.int32, (blocks, blocks), 0) < lax.broadcasted_iota(
        jnp.int32, (blocks, blocks), 1
    )
    again = jnp.where(earlier & (down_ref[...] == across_ref[...]), 1, 0)
    slots = across_ref[...] * 2 + jnp.sum(again, axis=0, keepdims=True)
    row = lax.broadcasted_iota(jnp.int32, (blocks, rows), 1)
    spread = row // block_rows == lax.broadcasted_iota(jnp.int32, (blocks, rows), 0)
    slots = jnp.broadcast_to(slots.astype(jnp.float32), (8, blocks)).astype(jnp.bfloat16)
    spread = jnp.where(spread, 1.0, 0.0).astype(jnp.bfloat16)
    slots = jnp.dot(slots, spread, preferred_element_type=jnp.float32)[:1].astype(jnp.int32)
    slots = slots * block_rows + row[:1] % block_rows
    shape = (out_ref.shape[0], rows)
    chosen = slots == lax.broadcasted_iota(jnp.int32, shape, 0)
    selector = jnp.where(chosen, 1.0, 0.0).astype(jnp.bfloat16)
    stores = []
    for d in range(4):
        fetches[d].wait()
        placed = jnp.dot(selector, rows_ref[d], preferred_element_type=jnp.float32)
        if marked and d == 0:
            used = jnp.sum(jnp.where(chosen, 1.0, 0.0), axis=1, keepdims=True)
            column = lax.broadcasted_iota(jnp.int32, placed.shape, 1)
            placed = placed + jnp.where(column == 0, MARK * (1.0 - used), 0.0)
        placed_ref[d] = placed.astype(jnp.bfloat16)
        store = pltpu.make_async_copy(
            placed_ref.at[d], out_ref.at[:, d * wide : (d + 1) * wide], out_sem.at[d]
        )
        store.start()
        stores.append(store)
    for store in stores:
        store.wait()


def pack(activations, targets, rows, start, wide, marked):
    hbm, vmem = pl.BlockSpec(memory_space=pltpu.HBM), pl.BlockSpec(memory_space=pltpu.VMEM)
    return pl.pallas_call(
        functools.partial(pack_kernel, marked, start),
        out_shape=jax.ShapeDtypeStruct((rows, 4 * wide), jnp.bfloat16),
        in_specs=[vmem, vmem, hbm],
        out_specs=hbm,
        scratch_shapes=[
            pltpu.VMEM((4, activations.shape[0], wide), jnp.bfloat16),
            pltpu.VMEM((4, rows, wide), jnp.bfloat16),
            pltpu.SemaphoreType.DMA((4,)),
            pltpu.SemaphoreType.DMA((4,)),
        ],
        compiler_params=pltpu.CompilerParams(vmem_limit_bytes=60 * 1024 * 1024),
    )(targets.reshape(1, -1), targets.reshape(-1, 1), activations)


def copies(pieces, sem):
    started = []
    for i, (source, target) in enumerate(pieces):
        copy = pltpu.make_async_copy(source, target, sem.at[i])
        copy.start()
        started.append(copy)
    for copy in started:
        copy.wait()


def place_first(upper_ref, lower_ref, out_ref, sem):
    half, first = upper_ref.shape[0], upper_ref.shape[1] // 4
    strip = out_ref.shape[1] // 4
    copies(
        [
            (
                ref.at[:, d * first : (d + 1) * first],
                out_ref.at[h * half : (h + 1) * half, d * strip : d * strip + first],
            )
            for h, ref in enumerate((upper_ref, lower_ref))
            for d in range(4)
        ],
        sem,
    )


def place_second(upper_ref, lower_ref, before_ref, out_ref, sem):
    rows, last = upper_ref.shape[0], upper_ref.shape[1] // 4
    strip = out_ref.shape[1] // 4
    first, half = strip - last, last // 2
    pieces = []
    for d in range(4):
        column = slice(d * strip + first, (d + 1) * strip)
        pieces.append((upper_ref.at[:, d * last : (d + 1) * last], out_ref.at[:rows, column]))
        pieces.append((lower_ref.at[:half, d * last : (d + 1) * last], out_ref.at[rows:, column]))
        for j in range(4 * first // 512):
            left, right = max(d * first, 512 * j), min((d + 1) * first, 512 * (j + 1))
            if left < right:
                row = half + last * j
                source = lower_ref.at[row : row + last, left - 512 * j : right - 512 * j]
                column = d * strip - d * first
                pieces.append((source, out_ref.at[first:, left + column : right + column]))
    copies(pieces, sem)


def place(kernel, shape, upper, lower, *before):
    hbm, vmem = pl.BlockSpec(memory_space=pltpu.HBM), pl.BlockSpec(memory_space=pltpu.VMEM)
    return pl.pallas_call(
        kernel,
        out_shape=jax.ShapeDtypeStruct(shape, jnp.float32),
        in_specs=[vmem, vmem] + [hbm] * len(before),
        out_specs=hbm,
        input_output_aliases={2: 0} if before else {},
        scratch_shapes=[pltpu.SemaphoreType.DMA((16,))],
        compiler_params=pltpu.CompilerParams(vmem_limit_bytes=24 * 1024 * 1024),
    )(upper, lower, *before)


def fourth(value):
    return (value * value) * (value * value)


def note_of(got):
    rows = got.shape[0] - NOTE
    return tuple(got[rows + i : rows + i + 1].astype(jnp.float32) for i in range(3))


class Ring:
    def __init__(self, far, grams, ranks):
        self.ranks = ranks
        upper, lower, facts = far()
        self.far = self.send(upper, 1), self.send(lower, -1)
        behind, ahead = grams(facts, -1, 1)
        near = ahead.astype(WIRE), behind.astype(WIRE)
        self.direct = self.send(near[0], 1), self.send(near[1], -1)
        self.facts = facts
        far, facts, _ = lax.optimization_barrier((self.far, facts, near))
        ahead, behind = grams(facts, 1, -1)
        merged = self.merge(ahead, far[0]).astype(WIRE), self.merge(behind, far[1]).astype(WIRE)
        self.merged = self.send(merged[0], 1), self.send(merged[1], -1)
        self.own = grams(facts, 0, 0)

    def send(self, values, step):
        pairs = [(i, (i + step) % self.ranks) for i in range(self.ranks)]
        return lax.ppermute(values.astype(WIRE), "blk", pairs)

    def merge(self, mine, got):
        got_coarse, got_fine, got_count = note_of(got)
        coarse, fine, count = note_of(mine)
        got_unit, unit = fourth(got_coarse * got_fine), fourth(coarse * fine)
        larger = jnp.maximum(unit, got_unit)
        row = lax.broadcasted_iota(jnp.int32, mine.shape, 0)
        rows = mine.shape[0] - NOTE
        both = mine * (unit / larger) + got.astype(jnp.float32) * (got_unit / larger)
        coarse = jnp.where(got_unit > unit, got_coarse, coarse)
        fine = jnp.where(got_unit > unit, got_fine, fine)
        note = jnp.where(row == rows, coarse, jnp.where(row == rows + 1, fine, count + got_count))
        return jnp.where(row < rows, both, note)

    def total(self):
        own = self.own
        rows = own[0].shape[0] - NOTE
        halves = []
        for mine, parts in (
            (own[0], (self.merged[0], self.direct[1])),
            (own[1], (self.direct[0], self.merged[1])),
        ):
            value = 0.0
            count = 0.0
            for got in (mine,) + parts:
                coarse, fine, more = note_of(got)
                value = value + got[:rows].astype(jnp.float32) * fourth(coarse * fine)
                count = count + more
            halves.append(value * (1.0 / TOP))
        return halves, count


def on_device(activations, destination):
    block_count = destination.shape[0]
    rows, width = activations.shape
    block_rows = rows // block_count
    groups = lax.axis_size("expert")
    ranks = lax.axis_size("blk")
    strip = width // ranks
    last = strip - FIRST
    capacity = 2
    slot_rows = groups * capacity * block_rows
    me = lax.axis_index("blk")

    def packed(start, stop, marked):
        placed = pack(activations, destination, slot_rows, start, stop - start, marked)
        return placed.reshape(groups, capacity * block_rows, placed.shape[1])

    def routed(x):
        got = lax.all_to_all(x, "expert", split_axis=0, concat_axis=0, tiled=True)
        return got.reshape(slot_rows, got.shape[2])

    def owners(offsets):
        return jnp.stack([lax.rem(me + o + ranks, ranks) for o in offsets])

    x0 = routed(packed(0, FIRST, True))
    x0, later = lax.optimization_barrier((x0, packed(FIRST, strip, False)))
    x1 = routed(later)

    corner = x0[:, :128]
    is_mark = (corner > MARK / 2) & (lax.broadcasted_iota(jnp.int32, corner.shape, 1) == 0)
    x0 = lax.dynamic_update_slice(x0, jnp.where(is_mark, jnp.zeros_like(corner), corner), (0, 0))

    def owners(offsets):
        return jnp.stack([lax.rem(me + o + ranks, ranks) for o in offsets])

    x0 = routed(packed(0, FIRST, True))
    x0, later = lax.optimization_barrier((x0, packed(FIRST, strip, False)))
    x1 = routed(later)

    corner = x0[:, :128]
    is_mark = (corner > MARK / 2) & (lax.broadcasted_iota(jnp.int32, corner.shape, 1) == 0)
    empty_blocks = jnp.sum(is_mark.astype(jnp.float32)) / block_rows
    x0 = lax.dynamic_update_slice(x0, jnp.where(is_mark, jnp.zeros_like(corner), corner), (0, 0))

    half0, half1 = FIRST // 2, FIRST + last // 2
    ring0 = Ring(
        lambda: partial_grams(
            first_far, half0, ranks * FIRST, owners((2, 2)), corner, x0, facts=True
        ),
        lambda facts, *offsets: partial_grams(
            first_body, half0, ranks * FIRST, owners(offsets), facts, x0
        ),
        ranks,
    )
    (ring0.direct, ring0.merged), x1 = lax.optimization_barrier(
        ((ring0.direct, ring0.merged), x1)
    )
    ring1 = Ring(
        lambda: partial_grams(
            second_far, half1, ranks * last, owners((2, 2)), ring0.facts, x0, x1, facts=True
        ),
        lambda facts, *offsets: partial_grams(
            second_body, half1, ranks * last, owners(offsets), facts, x0, x1
        ),
        ranks,
    )

    ring0.merged, _ = lax.optimization_barrier((ring0.merged, ring1.facts))
    sums0, empty_blocks = ring0.total()
    hessian_scale = 2.0 / (float(ranks * slot_rows) - block_rows * empty_blocks)
    shape = (strip, width)
    out = place(place_first, shape, *[half * hessian_scale for half in sums0])
    sums1, _ = ring1.total()
    hessian_scale = hessian_scale[:, : ranks * last]
    out = place(place_second, shape, *[half * hessian_scale for half in sums1], out)
    return out[None]


def solution(mesh):
    in_specs = (P(("expert", "blk"), None), P(("expert", "blk"), None))
    out_specs = P("expert", "blk", None)
    return jax.shard_map(
        on_device, mesh=mesh, in_specs=in_specs, out_specs=out_specs, check_vma=False
    )
```

```python
import functools
import math

import jax
import jax.numpy as jnp
from jax import lax
from jax.experimental import pallas as pl
from jax.experimental.pallas import tpu as pltpu
from jax.sharding import PartitionSpec as P

FIRST = 384
WIRE = jnp.float16
NOTE = 16
MARK = 64.0
TOP = 8192.0


def rows_dot(left, right):
    return lax.dot_general(
        left, right, (((0,), (0,)), ((), ())), preferred_element_type=jnp.float32
    )


def top_of(x_ref):
    tops = [
        jnp.max(jnp.abs(x_ref[:, 512 * j : 512 * (j + 1)]), axis=0, keepdims=True)
        for j in range(x_ref.shape[1] // 512)
    ]
    top = tops[0]
    for other in tops[1:]:
        top = jnp.maximum(top, other)
    return jnp.maximum(jnp.max(top.astype(jnp.float32), axis=1, keepdims=True), 1e-12)


def write_facts(facts_ref, top, rows, count):
    quarter = jnp.ceil((0.5 / math.log(2.0)) * jnp.log(top) + 1e-3 + 0.25 * rows.bit_length())
    coarse = jnp.clip(quarter, -14.0, 15.0)
    fine = jnp.clip(quarter - coarse, -14.0, 0.0)
    row = lax.broadcasted_iota(jnp.int32, facts_ref.shape, 0)
    unit = jnp.where(row == 1, jnp.exp2(coarse), jnp.exp2(fine))
    facts_ref[...] = jnp.where(row == 0, top, jnp.where(row < 3, unit, count))


def scale_and_notes(facts_ref, *out_refs):
    coarse, fine, count = facts_ref[1:2, :1], facts_ref[2:3, :1], facts_ref[3:4, :1]
    for ref in out_refs:
        row = lax.broadcasted_iota(jnp.int32, (NOTE, ref.shape[1]), 0)
        note = jnp.where(row == 0, coarse, jnp.where(row == 1, fine, count))
        ref[ref.shape[0] - NOTE :, :] = note
    return TOP / fourth(coarse * fine)


def first_body(owners_ref, facts_ref, x0_ref, upper_ref, lower_ref):
    first = x0_ref.shape[1] // 4
    half = first // 2
    scale = scale_and_notes(facts_ref, upper_ref, lower_ref)
    for h, ref in enumerate((upper_ref, lower_ref)):
        left = x0_ref[:, pl.ds(pl.multiple_of(owners_ref[h] * first, 128), first)]
        left = left[:, h * half : (h + 1) * half]
        for j in range(x0_ref.shape[1] // 512):
            block = rows_dot(left, x0_ref[:, 512 * j : 512 * (j + 1)])
            ref[:half, 512 * j : 512 * (j + 1)] = block * scale


def second_body(owners_ref, facts_ref, x0_ref, x1_ref, upper_ref, lower_ref):
    first = x0_ref.shape[1] // 4
    last = x1_ref.shape[1] // 4
    half = last // 2
    scale = scale_and_notes(facts_ref, upper_ref, lower_ref)
    left0 = x0_ref[:, pl.ds(pl.multiple_of(owners_ref[0] * first, 128), first)]
    left1 = x1_ref[:, pl.ds(pl.multiple_of(owners_ref[0] * last, 128), last)]
    upper_ref[:first] = rows_dot(left0, x1_ref[...]) * scale
    upper_ref[first : first + half] = rows_dot(left1, x1_ref[...])[:half] * scale
    left1 = x1_ref[:, pl.ds(pl.multiple_of(owners_ref[1] * last, 128), last)]
    lower_ref[:half] = rows_dot(left1, x1_ref[...])[half:] * scale
    for j in range(x0_ref.shape[1] // 512):
        block = rows_dot(left1, x0_ref[:, 512 * j : 512 * (j + 1)])
        lower_ref[half + last * j : half + last * (j + 1)] = block * scale


def first_far(owners_ref, corner_ref, x0_ref, upper_ref, lower_ref, facts_ref):
    marks = jnp.where(corner_ref[:, :1].astype(jnp.float32) > MARK / 2, 1.0 / 8.0, 0.0)
    count = jnp.sum(marks, axis=0, keepdims=True)
    write_facts(facts_ref, top_of(x0_ref), x0_ref.shape[0], count)
    first_body(owners_ref, facts_ref, x0_ref, upper_ref, lower_ref)


def second_far(owners_ref, before_ref, x0_ref, x1_ref, upper_ref, lower_ref, facts_ref):
    top = jnp.maximum(before_ref[:1, :1], top_of(x1_ref))
    write_facts(facts_ref, top, x0_ref.shape[0], jnp.zeros_like(top))
    second_body(owners_ref, facts_ref, x0_ref, x1_ref, upper_ref, lower_ref)


def partial_grams(kernel, rows, wide, owners, *arrays, facts=False):
    smem = pl.BlockSpec(memory_space=pltpu.SMEM)
    vmem = pl.BlockSpec(memory_space=pltpu.VMEM)
    shapes = [jax.ShapeDtypeStruct((rows + NOTE, wide), jnp.float32)] * 2
    shapes += [jax.ShapeDtypeStruct((8, 128), jnp.float32)] * facts
    return pl.pallas_call(
        kernel,
        out_shape=shapes,
        in_specs=[smem] + [vmem] * len(arrays),
        out_specs=[vmem] * len(shapes),
        compiler_params=pltpu.CompilerParams(vmem_limit_bytes=40 * 1024 * 1024),
        cost_estimate=pl.CostEstimate(flops=0, bytes_accessed=0, transcendentals=0),
    )(owners, *arrays)


def pack_kernel(
    marked, start, across_ref, down_ref, activations_ref, out_ref, rows_ref, placed_ref, in_sem, out_sem
):
    strip = activations_ref.shape[1] // 4
    wide = out_ref.shape[1] // 4
    fetches = [
        pltpu.make_async_copy(
            activations_ref.at[:, d * strip + start : d * strip + start + wide],
            rows_ref.at[d],
            in_sem.at[d],
        )
        for d in range(4)
    ]
    for fetch in fetches:
        fetch.start()
    blocks, rows = across_ref.shape[1], activations_ref.shape[0]
    block_rows = rows // blocks
    earlier = lax.broadcasted_iota(jnp.int32, (blocks, blocks), 0) < lax.broadcasted_iota(
        jnp.int32, (blocks, blocks), 1
    )
    again = jnp.where(earlier & (down_ref[...] == across_ref[...]), 1, 0)
    slots = across_ref[...] * 2 + jnp.sum(again, axis=0, keepdims=True)
    row = lax.broadcasted_iota(jnp.int32, (blocks, rows), 1)
    spread = row // block_rows == lax.broadcasted_iota(jnp.int32, (blocks, rows), 0)
    slots = jnp.broadcast_to(slots.astype(jnp.float32), (8, blocks)).astype(jnp.bfloat16)
    spread = jnp.where(spread, 1.0, 0.0).astype(jnp.bfloat16)
    slots = jnp.dot(slots, spread, preferred_element_type=jnp.float32)[:1].astype(jnp.int32)
    slots = slots * block_rows + row[:1] % block_rows
    shape = (out_ref.shape[0], rows)
    chosen = slots == lax.broadcasted_iota(jnp.int32, shape, 0)
    selector = jnp.where(chosen, 1.0, 0.0).astype(jnp.bfloat16)
    stores = []
    for d in range(4):
        fetches[d].wait()
        placed = jnp.dot(selector, rows_ref[d], preferred_element_type=jnp.float32)
        if marked and d == 0:
            used = jnp.sum(jnp.where(chosen, 1.0, 0.0), axis=1, keepdims=True)
            column = lax.broadcasted_iota(jnp.int32, placed.shape, 1)
            placed = placed + jnp.where(column == 0, MARK * (1.0 - used), 0.0)
        placed_ref[d] = placed.astype(jnp.bfloat16)
        store = pltpu.make_async_copy(
            placed_ref.at[d], out_ref.at[:, d * wide : (d + 1) * wide], out_sem.at[d]
        )
        store.start()
        stores.append(store)
    for store in stores:
        store.wait()


def pack(activations, targets, rows, start, wide, marked):
    hbm, vmem = pl.BlockSpec(memory_space=pltpu.HBM), pl.BlockSpec(memory_space=pltpu.VMEM)
    return pl.pallas_call(
        functools.partial(pack_kernel, marked, start),
        out_shape=jax.ShapeDtypeStruct((rows, 4 * wide), jnp.bfloat16),
        in_specs=[vmem, vmem, hbm],
        out_specs=hbm,
        scratch_shapes=[
            pltpu.VMEM((4, activations.shape[0], wide), jnp.bfloat16),
            pltpu.VMEM((4, rows, wide), jnp.bfloat16),
            pltpu.SemaphoreType.DMA((4,)),
            pltpu.SemaphoreType.DMA((4,)),
        ],
        compiler_params=pltpu.CompilerParams(vmem_limit_bytes=60 * 1024 * 1024),
    )(targets.reshape(1, -1), targets.reshape(-1, 1), activations)


def copies(pieces, sem):
    started = []
    for i, (source, target) in enumerate(pieces):
        copy = pltpu.make_async_copy(source, target, sem.at[i])
        copy.start()
        started.append(copy)
    for copy in started:
        copy.wait()


def place_first(upper_ref, lower_ref, out_ref, sem):
    half, first = upper_ref.shape[0], upper_ref.shape[1] // 4
    strip = out_ref.shape[1] // 4
    copies(
        [
            (
                ref.at[:, d * first : (d + 1) * first],
                out_ref.at[h * half : (h + 1) * half, d * strip : d * strip + first],
            )
            for h, ref in enumerate((upper_ref, lower_ref))
            for d in range(4)
        ],
        sem,
    )


def place_second(upper_ref, lower_ref, before_ref, out_ref, sem):
    rows, last = upper_ref.shape[0], upper_ref.shape[1] // 4
    strip = out_ref.shape[1] // 4
    first, half = strip - last, last // 2
    pieces = []
    for d in range(4):
        column = slice(d * strip + first, (d + 1) * strip)
        pieces.append((upper_ref.at[:, d * last : (d + 1) * last], out_ref.at[:rows, column]))
        pieces.append((lower_ref.at[:half, d * last : (d + 1) * last], out_ref.at[rows:, column]))
        for j in range(4 * first // 512):
            left, right = max(d * first, 512 * j), min((d + 1) * first, 512 * (j + 1))
            if left < right:
                row = half + last * j
                source = lower_ref.at[row : row + last, left - 512 * j : right - 512 * j]
                column = d * strip - d * first
                pieces.append((source, out_ref.at[first:, left + column : right + column]))
    copies(pieces, sem)


def place(kernel, shape, upper, lower, *before):
    hbm, vmem = pl.BlockSpec(memory_space=pltpu.HBM), pl.BlockSpec(memory_space=pltpu.VMEM)
    return pl.pallas_call(
        kernel,
        out_shape=jax.ShapeDtypeStruct(shape, jnp.float32),
        in_specs=[vmem, vmem] + [hbm] * len(before),
        out_specs=hbm,
        input_output_aliases={2: 0} if before else {},
        scratch_shapes=[pltpu.SemaphoreType.DMA((16,))],
        compiler_params=pltpu.CompilerParams(vmem_limit_bytes=24 * 1024 * 1024),
    )(upper, lower, *before)


def fourth(value):
    return (value * value) * (value * value)


def note_of(got):
    rows = got.shape[0] - NOTE
    return tuple(got[rows + i : rows + i + 1].astype(jnp.float32) for i in range(3))


class Ring:
    def __init__(self, far, grams, ranks):
        self.ranks = ranks
        upper, lower, facts = far()
        self.far = self.send(upper, 1), self.send(lower, -1)
        behind, ahead = grams(facts, -1, 1)
        near = ahead.astype(WIRE), behind.astype(WIRE)
        self.direct = self.send(near[0], 1), self.send(near[1], -1)
        self.facts = facts
        far, facts, _ = lax.optimization_barrier((self.far, facts, near))
        ahead, behind = grams(facts, 1, -1)
        self.passed = self.merge(ahead, far[0]).astype(WIRE), self.merge(behind, far[1]).astype(WIRE)
        self.merged = self.send(self.passed[0], 1), self.send(self.passed[1], -1)
        self.own = grams(facts, 0, 0)

    def send(self, values, step):
        pairs = [(i, (i + step) % self.ranks) for i in range(self.ranks)]
        return lax.ppermute(values.astype(WIRE), "blk", pairs)

    def merge(self, mine, got):
        got_coarse, got_fine, got_count = note_of(got)
        coarse, fine, count = note_of(mine)
        got_unit, unit = fourth(got_coarse * got_fine), fourth(coarse * fine)
        larger = jnp.maximum(unit, got_unit)
        row = lax.broadcasted_iota(jnp.int32, mine.shape, 0)
        rows = mine.shape[0] - NOTE
        both = mine * (unit / larger) + got.astype(jnp.float32) * (got_unit / larger)
        coarse = jnp.where(got_unit > unit, got_coarse, coarse)
        fine = jnp.where(got_unit > unit, got_fine, fine)
        note = jnp.where(row == rows, coarse, jnp.where(row == rows + 1, fine, count + got_count))
        return jnp.where(row < rows, both, note)

    def total(self):
        own = self.own
        rows = own[0].shape[0] - NOTE
        halves = []
        for mine, parts in (
            (own[0], (self.merged[0], self.direct[1])),
            (own[1], (self.direct[0], self.merged[1])),
        ):
            value = 0.0
            count = 0.0
            for got in (mine,) + parts:
                coarse, fine, more = note_of(got)
                value = value + got[:rows].astype(jnp.float32) * fourth(coarse * fine)
                count = count + more
            halves.append(value * (1.0 / TOP))
        return halves, count


def on_device(activations, destination):
    block_count = destination.shape[0]
    rows, width = activations.shape
    block_rows = rows // block_count
    groups = lax.axis_size("expert")
    ranks = lax.axis_size("blk")
    strip = width // ranks
    last = strip - FIRST
    capacity = 2
    slot_rows = groups * capacity * block_rows
    me = lax.axis_index("blk")

    def packed(start, stop, marked):
        placed = pack(activations, destination, slot_rows, start, stop - start, marked)
        return placed.reshape(groups, capacity * block_rows, placed.shape[1])

    def routed(x):
        got = lax.all_to_all(x, "expert", split_axis=0, concat_axis=0, tiled=True)
        return got.reshape(slot_rows, got.shape[2])

    def owners(offsets):
        return jnp.stack([lax.rem(me + o + ranks, ranks) for o in offsets])

    x0 = routed(packed(0, FIRST, True))
    x0, later = lax.optimization_barrier((x0, packed(FIRST, strip, False)))
    x1 = routed(later)

    corner = x0[:, :128]
    is_mark = (corner > MARK / 2) & (lax.broadcasted_iota(jnp.int32, corner.shape, 1) == 0)
    x0 = lax.dynamic_update_slice(x0, jnp.where(is_mark, jnp.zeros_like(corner), corner), (0, 0))

    half0, half1 = FIRST // 2, FIRST + last // 2
    ring0 = Ring(
        lambda: partial_grams(
            first_far, half0, ranks * FIRST, owners((2, 2)), corner, x0, facts=True
        ),
        lambda facts, *offsets: partial_grams(
            first_body, half0, ranks * FIRST, owners(offsets), facts, x0
        ),
        ranks,
    )
    ring0.direct, _, x1 = lax.optimization_barrier((ring0.direct, ring0.passed, x1))
    ring1 = Ring(
        lambda: partial_grams(
            second_far, half1, ranks * last, owners((2, 2)), ring0.facts, x0, x1, facts=True
        ),
        lambda facts, *offsets: partial_grams(
            second_body, half1, ranks * last, owners(offsets), facts, x0, x1
        ),
        ranks,
    )

    ring0.merged, _ = lax.optimization_barrier((ring0.merged, ring1.facts))
    sums0, empty_blocks = ring0.total()
    hessian_scale = 2.0 / (float(ranks * slot_rows) - block_rows * empty_blocks)
    shape = (strip, width)
    out = place(place_first, shape, *[half * hessian_scale for half in sums0])
    sums1, _ = ring1.total()
    hessian_scale = hessian_scale[:, : ranks * last]
    out = place(place_second, shape, *[half * hessian_scale for half in sums1], out)
    return out[None]


def solution(mesh):
    in_specs = (P(("expert", "blk"), None), P(("expert", "blk"), None))
    out_specs = P("expert", "blk", None)
    return jax.shard_map(
        on_device, mesh=mesh, in_specs=in_specs, out_specs=out_specs, check_vma=False
    )
```

```python
import functools
import math

import jax
import jax.numpy as jnp
from jax import lax
from jax.experimental import pallas as pl
from jax.experimental.pallas import tpu as pltpu
from jax.sharding import PartitionSpec as P

FIRST = 384
WIRE = jnp.float16
NOTE = 16
MARK = 64.0
TOP = 8192.0


def rows_dot(left, right):
    return lax.dot_general(
        left, right, (((0,), (0,)), ((), ())), preferred_element_type=jnp.float32
    )


def top_of(x_ref):
    tops = [
        jnp.max(jnp.abs(x_ref[:, 512 * j : 512 * (j + 1)]), axis=0, keepdims=True)
        for j in range(x_ref.shape[1] // 512)
    ]
    top = tops[0]
    for other in tops[1:]:
        top = jnp.maximum(top, other)
    return jnp.maximum(jnp.max(top.astype(jnp.float32), axis=1, keepdims=True), 1e-12)


def write_facts(facts_ref, top, rows, count):
    quarter = jnp.ceil((0.5 / math.log(2.0)) * jnp.log(top) + 1e-3 + 0.25 * rows.bit_length())
    coarse = jnp.clip(quarter, -14.0, 15.0)
    fine = jnp.clip(quarter - coarse, -14.0, 0.0)
    row = lax.broadcasted_iota(jnp.int32, facts_ref.shape, 0)
    unit = jnp.where(row == 1, jnp.exp2(coarse), jnp.exp2(fine))
    facts_ref[...] = jnp.where(row == 0, top, jnp.where(row < 3, unit, count))


def scale_and_notes(facts_ref, *out_refs):
    coarse, fine, count = facts_ref[1:2, :1], facts_ref[2:3, :1], facts_ref[3:4, :1]
    for ref in out_refs:
        row = lax.broadcasted_iota(jnp.int32, (NOTE, ref.shape[1]), 0)
        note = jnp.where(row == 0, coarse, jnp.where(row == 1, fine, count))
        ref[ref.shape[0] - NOTE :, :] = note
    return TOP / fourth(coarse * fine)


def first_body(owners_ref, facts_ref, x0_ref, upper_ref, lower_ref):
    first = x0_ref.shape[1] // 4
    half = first // 2
    scale = scale_and_notes(facts_ref, upper_ref, lower_ref)
    for h, ref in enumerate((upper_ref, lower_ref)):
        own = x0_ref[:, pl.ds(pl.multiple_of(owners_ref[h] * first, 128), first)]
        if h == 0:
            ref[:128, :256] = rows_dot(own[:, :128], own[:, :256]) * scale
            ref[128:half, :256] = rows_dot(own[:, 128:half], own[:, 128:]) * scale
        else:
            ref[:64, :256] = rows_dot(own[:, half:256], own[:, 128:]) * scale
            ref[64:half, :128] = rows_dot(own[:, 256:], own[:, 256:]) * scale
            ref[64:half, 128:256] = rows_dot(own[:, 256:], own[:, :128]) * scale
        left = own[:, h * half : (h + 1) * half]
        for r in range(1, 4):
            other = pl.multiple_of(lax.rem(owners_ref[h] + r, 4) * first, 128)
            block = rows_dot(left, x0_ref[:, pl.ds(other, first)])
            ref[:half, 256 + first * (r - 1) : 256 + first * r] = block * scale


def second_body(owners_ref, facts_ref, x0_ref, x1_ref, upper_ref, lower_ref):
    first = x0_ref.shape[1] // 4
    last = x1_ref.shape[1] // 4
    half = last // 2
    scale = scale_and_notes(facts_ref, upper_ref, lower_ref)
    left0 = x0_ref[:, pl.ds(pl.multiple_of(owners_ref[0] * first, 128), first)]
    left1 = x1_ref[:, pl.ds(pl.multiple_of(owners_ref[0] * last, 128), last)]
    upper_ref[:first] = rows_dot(left0, x1_ref[...]) * scale
    upper_ref[first : first + half] = rows_dot(left1, x1_ref[...])[:half] * scale
    left1 = x1_ref[:, pl.ds(pl.multiple_of(owners_ref[1] * last, 128), last)]
    lower_ref[:half] = rows_dot(left1, x1_ref[...])[half:] * scale
    for j in range(x0_ref.shape[1] // 512):
        block = rows_dot(left1, x0_ref[:, 512 * j : 512 * (j + 1)])
        lower_ref[half + last * j : half + last * (j + 1)] = block * scale


def first_far(owners_ref, corner_ref, x0_ref, upper_ref, lower_ref, facts_ref):
    marks = jnp.where(corner_ref[:, :1].astype(jnp.float32) > MARK / 2, 1.0 / 8.0, 0.0)
    count = jnp.sum(marks, axis=0, keepdims=True)
    write_facts(facts_ref, top_of(x0_ref), x0_ref.shape[0], count)
    first_body(owners_ref, facts_ref, x0_ref, upper_ref, lower_ref)


def second_far(owners_ref, before_ref, x0_ref, x1_ref, upper_ref, lower_ref, facts_ref):
    top = jnp.maximum(before_ref[:1, :1], top_of(x1_ref))
    write_facts(facts_ref, top, x0_ref.shape[0], jnp.zeros_like(top))
    second_body(owners_ref, facts_ref, x0_ref, x1_ref, upper_ref, lower_ref)


def partial_grams(kernel, rows, wide, owners, *arrays, facts=False):
    smem = pl.BlockSpec(memory_space=pltpu.SMEM)
    vmem = pl.BlockSpec(memory_space=pltpu.VMEM)
    shapes = [jax.ShapeDtypeStruct((rows + NOTE, wide), jnp.float32)] * 2
    shapes += [jax.ShapeDtypeStruct((8, 128), jnp.float32)] * facts
    return pl.pallas_call(
        kernel,
        out_shape=shapes,
        in_specs=[smem] + [vmem] * len(arrays),
        out_specs=[vmem] * len(shapes),
        compiler_params=pltpu.CompilerParams(vmem_limit_bytes=40 * 1024 * 1024),
        cost_estimate=pl.CostEstimate(
            flops=2000000000 if kernel is first_body else 0, bytes_accessed=0, transcendentals=0
        ),
    )(owners, *arrays)


def pack_kernel(
    marked, start, across_ref, down_ref, activations_ref, out_ref, rows_ref, placed_ref, in_sem, out_sem
):
    strip = activations_ref.shape[1] // 4
    wide = out_ref.shape[1] // 4
    fetches = [
        pltpu.make_async_copy(
            activations_ref.at[:, d * strip + start : d * strip + start + wide],
            rows_ref.at[d],
            in_sem.at[d],
        )
        for d in range(4)
    ]
    for fetch in fetches:
        fetch.start()
    blocks, rows = across_ref.shape[1], activations_ref.shape[0]
    block_rows = rows // blocks
    earlier = lax.broadcasted_iota(jnp.int32, (blocks, blocks), 0) < lax.broadcasted_iota(
        jnp.int32, (blocks, blocks), 1
    )
    again = jnp.where(earlier & (down_ref[...] == across_ref[...]), 1, 0)
    slots = across_ref[...] * 2 + jnp.sum(again, axis=0, keepdims=True)
    row = lax.broadcasted_iota(jnp.int32, (blocks, rows), 1)
    spread = row // block_rows == lax.broadcasted_iota(jnp.int32, (blocks, rows), 0)
    slots = jnp.broadcast_to(slots.astype(jnp.float32), (8, blocks)).astype(jnp.bfloat16)
    spread = jnp.where(spread, 1.0, 0.0).astype(jnp.bfloat16)
    slots = jnp.dot(slots, spread, preferred_element_type=jnp.float32)[:1].astype(jnp.int32)
    slots = slots * block_rows + row[:1] % block_rows
    shape = (out_ref.shape[0], rows)
    chosen = slots == lax.broadcasted_iota(jnp.int32, shape, 0)
    selector = jnp.where(chosen, 1.0, 0.0).astype(jnp.bfloat16)
    stores = []
    for d in range(4):
        fetches[d].wait()
        placed = jnp.dot(selector, rows_ref[d], preferred_element_type=jnp.float32)
        if marked and d == 0:
            used = jnp.sum(jnp.where(chosen, 1.0, 0.0), axis=1, keepdims=True)
            column = lax.broadcasted_iota(jnp.int32, placed.shape, 1)
            placed = placed + jnp.where(column == 0, MARK * (1.0 - used), 0.0)
        placed_ref[d] = placed.astype(jnp.bfloat16)
        store = pltpu.make_async_copy(
            placed_ref.at[d], out_ref.at[:, d * wide : (d + 1) * wide], out_sem.at[d]
        )
        store.start()
        stores.append(store)
    for store in stores:
        store.wait()


def pack(activations, targets, rows, start, wide, marked):
    hbm, vmem = pl.BlockSpec(memory_space=pltpu.HBM), pl.BlockSpec(memory_space=pltpu.VMEM)
    return pl.pallas_call(
        functools.partial(pack_kernel, marked, start),
        out_shape=jax.ShapeDtypeStruct((rows, 4 * wide), jnp.bfloat16),
        in_specs=[vmem, vmem, hbm],
        out_specs=hbm,
        scratch_shapes=[
            pltpu.VMEM((4, activations.shape[0], wide), jnp.bfloat16),
            pltpu.VMEM((4, rows, wide), jnp.bfloat16),
            pltpu.SemaphoreType.DMA((4,)),
            pltpu.SemaphoreType.DMA((4,)),
        ],
        compiler_params=pltpu.CompilerParams(vmem_limit_bytes=60 * 1024 * 1024),
    )(targets.reshape(1, -1), targets.reshape(-1, 1), activations)


def copies(pieces, sem):
    started = []
    for i, (source, target) in enumerate(pieces):
        copy = pltpu.make_async_copy(source, target, sem.at[i])
        copy.start()
        started.append(copy)
    for copy in started:
        copy.wait()


def place_first(me_ref, upper_ref, lower_ref, out_ref, square_ref, sem):
    half = upper_ref.shape[0]
    first, strip = 2 * half, out_ref.shape[1] // 4
    square_ref[:128, :256] = upper_ref[:128, :256]
    square_ref[128:half, 128:] = upper_ref[128:, :256]
    square_ref[half:256, 128:] = lower_ref[:64, :256]
    square_ref[256:, 256:] = lower_ref[64:, :128]
    square_ref[256:, :128] = lower_ref[64:, 128:256]
    square_ref[128:256, :128] = square_ref[:128, 128:256].T
    square_ref[256:, 128:256] = square_ref[128:256, 256:].T
    square_ref[:128, 256:] = square_ref[256:, :128].T
    column = pl.multiple_of(me_ref[0] * strip, 128)
    pieces = [(square_ref, out_ref.at[:first, pl.ds(column, first)])]
    for r in range(1, 4):
        column = pl.multiple_of(lax.rem(me_ref[0] + r, 4) * strip, 128)
        for h, ref in enumerate((upper_ref, lower_ref)):
            source = ref.at[:, 256 + first * (r - 1) : 256 + first * r]
            rows = slice(h * half, (h + 1) * half)
            pieces.append((source, out_ref.at[rows, pl.ds(column, first)]))
    copies(pieces, sem)


def place_second(upper_ref, lower_ref, before_ref, out_ref, sem):
    rows, last = upper_ref.shape[0], upper_ref.shape[1] // 4
    strip = out_ref.shape[1] // 4
    first, half = strip - last, last // 2
    pieces = []
    for d in range(4):
        column = slice(d * strip + first, (d + 1) * strip)
        pieces.append((upper_ref.at[:, d * last : (d + 1) * last], out_ref.at[:rows, column]))
        pieces.append((lower_ref.at[:half, d * last : (d + 1) * last], out_ref.at[rows:, column]))
        for j in range(4 * first // 512):
            left, right = max(d * first, 512 * j), min((d + 1) * first, 512 * (j + 1))
            if left < right:
                row = half + last * j
                source = lower_ref.at[row : row + last, left - 512 * j : right - 512 * j]
                column = d * strip - d * first
                pieces.append((source, out_ref.at[first:, left + column : right + column]))
    copies(pieces, sem)


def place(kernel, shape, upper, lower, me=None, before=None):
    hbm, vmem = pl.BlockSpec(memory_space=pltpu.HBM), pl.BlockSpec(memory_space=pltpu.VMEM)
    smem = pl.BlockSpec(memory_space=pltpu.SMEM)
    scratch = [pltpu.SemaphoreType.DMA((16,))]
    if before is None:
        specs, arrays = [smem, vmem, vmem], (me.reshape(1), upper, lower)
        scratch = [pltpu.VMEM((FIRST, FIRST), jnp.float32)] + scratch
    else:
        specs, arrays = [vmem, vmem, hbm], (upper, lower, before)
    return pl.pallas_call(
        kernel,
        out_shape=jax.ShapeDtypeStruct(shape, jnp.float32),
        in_specs=specs,
        out_specs=hbm,
        input_output_aliases={} if before is None else {2: 0},
        scratch_shapes=scratch,
        compiler_params=pltpu.CompilerParams(vmem_limit_bytes=24 * 1024 * 1024),
    )(*arrays)


def fourth(value):
    return (value * value) * (value * value)


def note_of(got):
    rows = got.shape[0] - NOTE
    return tuple(got[rows + i : rows + i + 1].astype(jnp.float32) for i in range(3))


class Ring:
    def __init__(self, far, grams, ranks):
        self.ranks = ranks
        upper, lower, facts = far()
        self.far = self.send(upper, 1), self.send(lower, -1)
        behind, ahead = grams(facts, -1, 1)
        near = ahead.astype(WIRE), behind.astype(WIRE)
        self.direct = self.send(near[0], 1), self.send(near[1], -1)
        self.facts = facts
        far, facts, _ = lax.optimization_barrier((self.far, facts, near))
        ahead, behind = grams(facts, 1, -1)
        self.passed = self.merge(ahead, far[0]).astype(WIRE), self.merge(behind, far[1]).astype(WIRE)
        self.merged = self.send(self.passed[0], 1), self.send(self.passed[1], -1)
        self.own = grams(facts, 0, 0)

    def send(self, values, step):
        pairs = [(i, (i + step) % self.ranks) for i in range(self.ranks)]
        return lax.ppermute(values.astype(WIRE), "blk", pairs)

    def merge(self, mine, got):
        got_coarse, got_fine, got_count = note_of(got)
        coarse, fine, count = note_of(mine)
        got_unit, unit = fourth(got_coarse * got_fine), fourth(coarse * fine)
        larger = jnp.maximum(unit, got_unit)
        row = lax.broadcasted_iota(jnp.int32, mine.shape, 0)
        rows = mine.shape[0] - NOTE
        both = mine * (unit / larger) + got.astype(jnp.float32) * (got_unit / larger)
        coarse = jnp.where(got_unit > unit, got_coarse, coarse)
        fine = jnp.where(got_unit > unit, got_fine, fine)
        note = jnp.where(row == rows, coarse, jnp.where(row == rows + 1, fine, count + got_count))
        return jnp.where(row < rows, both, note)

    def total(self):
        own = self.own
        rows = own[0].shape[0] - NOTE
        halves = []
        for mine, parts in (
            (own[0], (self.merged[0], self.direct[1])),
            (own[1], (self.direct[0], self.merged[1])),
        ):
            value = 0.0
            count = 0.0
            for got in (mine,) + parts:
                coarse, fine, more = note_of(got)
                value = value + got[:rows].astype(jnp.float32) * fourth(coarse * fine)
                count = count + more
            halves.append(value * (1.0 / TOP))
        return halves, count


def on_device(activations, destination):
    block_count = destination.shape[0]
    rows, width = activations.shape
    block_rows = rows // block_count
    groups = lax.axis_size("expert")
    ranks = lax.axis_size("blk")
    strip = width // ranks
    last = strip - FIRST
    capacity = 2
    slot_rows = groups * capacity * block_rows
    me = lax.axis_index("blk")

    def packed(start, stop, marked):
        placed = pack(activations, destination, slot_rows, start, stop - start, marked)
        return placed.reshape(groups, capacity * block_rows, placed.shape[1])

    def routed(x):
        got = lax.all_to_all(x, "expert", split_axis=0, concat_axis=0, tiled=True)
        return got.reshape(slot_rows, got.shape[2])

    def owners(offsets):
        return jnp.stack([lax.rem(me + o + ranks, ranks) for o in offsets])

    x0 = routed(packed(0, FIRST, True))
    x0, later = lax.optimization_barrier((x0, packed(FIRST, strip, False)))
    x1 = routed(later)

    corner = x0[:, :128]
    is_mark = (corner > MARK / 2) & (lax.broadcasted_iota(jnp.int32, corner.shape, 1) == 0)
    x0 = lax.dynamic_update_slice(x0, jnp.where(is_mark, jnp.zeros_like(corner), corner), (0, 0))

    half0, half1 = FIRST // 2, FIRST + last // 2
    wide0 = 256 + (ranks - 1) * FIRST
    ring0 = Ring(
        lambda: partial_grams(
            first_far, half0, wide0, owners((2, 2)), corner, x0, facts=True
        ),
        lambda facts, *offsets: partial_grams(
            first_body, half0, wide0, owners(offsets), facts, x0
        ),
        ranks,
    )
    ring0.direct, _, x1 = lax.optimization_barrier((ring0.direct, ring0.passed, x1))
    ring1 = Ring(
        lambda: partial_grams(
            second_far, half1, ranks * last, owners((2, 2)), ring0.facts, x0, x1, facts=True
        ),
        lambda facts, *offsets: partial_grams(
            second_body, half1, ranks * last, owners(offsets), facts, x0, x1
        ),
        ranks,
    )

    ring0.merged, _ = lax.optimization_barrier((ring0.merged, ring1.facts))
    sums0, empty_blocks = ring0.total()
    hessian_scale = 2.0 / (float(ranks * slot_rows) - block_rows * empty_blocks)
    shape = (strip, width)
    out = place(place_first, shape, *[half * hessian_scale for half in sums0], me=me)
    sums1, _ = ring1.total()
    hessian_scale = hessian_scale[:, : ranks * last]
    out = place(place_second, shape, *[half * hessian_scale for half in sums1], before=out)
    return out[None]


def solution(mesh):
    in_specs = (P(("expert", "blk"), None), P(("expert", "blk"), None))
    out_specs = P("expert", "blk", None)
    return jax.shard_map(
        on_device, mesh=mesh, in_specs=in_specs, out_specs=out_specs, check_vma=False
    )
```
